32 devices in a mesh: parts: 2 (over y), req: 8 (over z, x), tensor: 2 (over core).
Axes of the slice: x: 2, y: 2, z: 4, core: 2. Of those that a mesh axis runs over, the one named last changes fastest.
Arguments:
- queries: bfloat16 [48, 64, 4096], P(('parts', 'req'), None, 'tensor'), parts along dimension 0, may hold values from -6 to 6
- block_keys: bfloat16 [48, 64, 512], P(('parts', 'req'), None, 'tensor'), parts along dimension 0, may hold values from -6 to 6
- block_values: bfloat16 [48, 64, 512], P(('parts', 'req'), None, 'tensor'), parts along dimension 0, may hold values from -6 to 6
- cache_keys: bfloat16 [48, 1024, 512], P(('parts', 'req'), None, 'tensor'), parts along dimension 0, may hold values from -6 to 6
- cache_values: bfloat16 [48, 1024, 512], P(('parts', 'req'), None, 'tensor'), parts along dimension 0, may hold values from -6 to 6
- block_len: int32 [16, 3], P(('parts', 'req')), parts along dimension 0, may hold values from 1 to 64, as said below
- prefix_len: int32 [16, 3], P(('parts', 'req')), parts along dimension 0, may hold values from 1 to 1024, as said below
- deferred: int32 [16, 3], P(('parts', 'req')), parts along dimension 0, may hold values 0 or 1
- route: int32 [16, 3], P(('parts', 'req')), parts along dimension 0, may hold values from 0 to 2, each once within a row
Outputs:
- attended: bfloat16 [48, 64, 4096], P(('parts', 'req'), None, 'tensor'), parts along dimension 0
The draws below stay inside these ranges and needn't reach their ends.
There are 2 independent parts, one for each index of `parts`. The reference program is written for one: setup_inputs(seed, part) draws one part's arguments, and reference() takes and returns one part's arrays. A program takes and returns all parts, laid end to end along the dimension named above; each array names one. Nothing has to cross between parts.
Inputs may be any that keep to these rules, and one draw needn't show every extreme that they name: `block_len`: live tokens of a prompt block; some block has all 64. `prefix_len`: live tokens of a cached prefix; some prefix has all 1024. `route`: each device's row holds every partner number once.
All inputs are finite; a program needn't handle non-finite values. No bound on the sum of `deferred` on one device may be relied on, other than what follows from the above.
Results may differ from the reference program's by a relative error of at most 0.0028.
Values may be sent and summed in bfloat16 or wider, within the bound.
A program may use at most 64 MiB of HBM per device.

```python
import jax
import jax.numpy as jnp
from jax import lax

HEADS = 32
KV_HEADS = 4
HEAD_DIM = 128
HOPS = 3
CL = 64
PREFIX = 1024
BLOCKS = 24
N_REQ = 8


def draw_queries(key, part):
    key = jax.random.fold_in(key, 21)
    shape = (BLOCKS, CL, HEADS * HEAD_DIM)
    values = jax.random.truncated_normal(key, -6.0, 6.0, shape, jnp.float32)
    return values.astype(jnp.bfloat16)


def draw_block_keys(key, part):
    key = jax.random.fold_in(key, 22)
    shape = (BLOCKS, CL, KV_HEADS * HEAD_DIM)
    values = jax.random.truncated_normal(key, -6.0, 6.0, shape, jnp.float32)
    return values.astype(jnp.bfloat16)


def draw_block_len(key, part):
    key = jax.random.fold_in(key, 11)
    first, second = jax.random.split(key)
    values = jax.random.randint(first, (N_REQ, HOPS), 1, CL + 1)
    spot = jax.random.randint(second, (), 0, N_REQ * HOPS)
    places = jnp.arange(N_REQ * HOPS).reshape(N_REQ, HOPS)
    return jnp.where(places == spot, CL, values).astype(jnp.int32)


def draw_prefix_len(key, part):
    key = jax.random.fold_in(key, 12)
    first, second = jax.random.split(key)
    values = jax.random.randint(first, (N_REQ, HOPS), 1, PREFIX + 1)
    spot = jax.random.randint(second, (), 0, N_REQ * HOPS)
    places = jnp.arange(N_REQ * HOPS).reshape(N_REQ, HOPS)
    return jnp.where(places == spot, PREFIX, values).astype(jnp.int32)


def set_ends(values, key, low, high):
    longest = values.shape.index(max(values.shape))
    spots = []
    for shift in (0, 1):
        where = [jax.random.randint(jax.random.fold_in(key, axis), (), 0, length) for axis, length in enumerate(values.shape)]
        where[longest] = (where[longest] + shift) % values.shape[longest]
        spots.append(tuple(where))
    return values.at[spots[0]].set(low).at[spots[1]].set(high)


def levels(rng, extent, cuts, low, largest):
    loudness, own = 1.0, jax.random.fold_in(rng, 6)
    for dim, blocks in cuts:
        draws = jnp.exp(jax.random.uniform(jax.random.fold_in(own, dim), (blocks,), jnp.float32, low / len(cuts), largest / len(cuts)))
        loudness = loudness * jnp.repeat(draws, extent[dim] // blocks).reshape([-1 if axis == dim else 1 for axis in range(len(extent))])
    return loudness


def noise(stream_key, extent, deviation, most, pieces=(), kind=jnp.bfloat16):
    values = deviation * jax.random.normal(stream_key, extent, jnp.float32)
    if pieces:
        values = values * levels(stream_key, extent, pieces, -0.22, 0.18)
    return jnp.clip(values, -most, most).astype(kind)


def setup_inputs(seed: int = 0, part: int = 0) -> dict:
    key_of = jax.random.split(jax.random.key(seed), 10)
    part_splits = jax.random.split(jax.random.fold_in(key_of[9], part), 10)
    return {
        "queries": draw_queries(jax.random.fold_in(jax.random.fold_in(key_of[9], part), 71), part),
        "block_keys": draw_block_keys(jax.random.fold_in(jax.random.fold_in(key_of[9], part), 71), part),
        "block_values": noise(part_splits[2], (BLOCKS, CL, KV_HEADS * HEAD_DIM), 1.0, 6.0, ((0, 8), (2, 2))),
        "cache_keys": noise(part_splits[3], (BLOCKS, PREFIX, KV_HEADS * HEAD_DIM), 1.0, 6.0, ((0, 8), (2, 2))),
        "cache_values": noise(part_splits[4], (BLOCKS, PREFIX, KV_HEADS * HEAD_DIM), 1.0, 6.0, ((0, 8), (2, 2))),
        "block_len": draw_block_len(jax.random.fold_in(jax.random.fold_in(key_of[9], part), 71), part),
        "prefix_len": draw_prefix_len(jax.random.fold_in(jax.random.fold_in(key_of[9], part), 71), part),
        "deferred": set_ends((jax.random.randint(part_splits[7], (N_REQ, HOPS), 0, 4) < 3).astype(jnp.int32), jax.random.fold_in(part_splits[7], 1), 0, 1),
        "route": jax.vmap(lambda own: jax.random.permutation(own, HOPS))(jax.random.split(part_splits[8], N_REQ)).reshape((N_REQ, HOPS)).astype(jnp.int32),
    }


def attend_full(query, block_key, block_value, cache_key, cache_value, cache_valid, row_valid):
    rows = query.shape[0]
    groups = block_key.shape[1] // HEAD_DIM
    ratio = query.shape[1] // HEAD_DIM // groups
    query_four = query.astype(jnp.float32).reshape(rows, groups, ratio, HEAD_DIM)
    keys_all = jnp.concatenate([cache_key, block_key], axis=0).astype(jnp.float32).reshape(-1, groups, HEAD_DIM)
    values_all = jnp.concatenate([cache_value, block_value], axis=0).astype(jnp.float32).reshape(-1, groups, HEAD_DIM)
    scores = jnp.einsum('igrd,jgd->grij', query_four, keys_all) / jnp.sqrt(jnp.float32(HEAD_DIM))
    position = jnp.arange(rows, dtype=jnp.int32)
    inner = (position[None, :] <= position[:, None]) & row_valid[None, :]
    outer = jnp.broadcast_to(cache_valid[None, :], (rows, cache_valid.shape[0]))
    visible = jnp.concatenate([outer, inner], axis=1)
    highest = lax.optimization_barrier(jnp.max(jnp.where(visible, scores, jnp.float32(-1e+30)), axis=-1, keepdims=True))
    weights = jnp.where(visible, jnp.exp(scores - highest), jnp.float32(0.0))
    totals = lax.optimization_barrier(jnp.sum(weights, axis=-1))
    rounded = weights.astype(jnp.bfloat16).astype(jnp.float32)
    mixed = jnp.einsum('grij,jgd->igrd', rounded, values_all) / jnp.transpose(totals, (2, 0, 1))[..., None]
    mixed = mixed.reshape(rows, -1)
    return jnp.where(row_valid[:, None], mixed, jnp.float32(0.0)).astype(jnp.bfloat16)

def reference(queries, block_keys, block_values, cache_keys, cache_values, block_len, prefix_len, deferred, route):
    distances = jnp.array([1, N_REQ // 4, N_REQ // 2], dtype=jnp.int32)
    anchor = jnp.arange(N_REQ, dtype=jnp.int32)[:, None]
    target = (anchor + distances[route]) % N_REQ
    slots = (target * HOPS + route).reshape(-1).astype(jnp.int32)
    prefix_for = prefix_len.reshape(-1)[slots]
    flags = deferred.reshape(-1)
    cache_valid = (jnp.arange(PREFIX, dtype=jnp.int32)[None, :] < prefix_for[:, None]) & (flags[:, None] == 1)
    row_valid = jnp.arange(CL, dtype=jnp.int32)[None, :] < block_len.reshape(-1)[:, None]

    def one_block(index):
        slot = slots[index]
        return attend_full(queries[index], block_keys[index], block_values[index], cache_keys[slot], cache_values[slot], cache_valid[index], row_valid[index])
    return lax.map(one_block, jnp.arange(N_REQ * HOPS, dtype=jnp.int32))
```

```python
import functools
import math

import jax
import jax.numpy as jnp
from jax import lax
from jax.experimental import pallas as pl
from jax.experimental.pallas import tpu as pltpu
from jax.sharding import PartitionSpec as P

HEAD_DIM = 128
LANES = 128
HIDDEN = -1e30
LEVELS = 32767.0
MESH = pl.DeviceIdType.MESH
SCALE = math.log2(math.e) / math.sqrt(HEAD_DIM)


def dot_nt(a, b):
    return lax.dot_general(a, b, (((1,), (1,)), ((), ())), preferred_element_type=jnp.float32)


def heads_to_lanes(column, rows, ratio, first, into):
    lane = lax.broadcasted_iota(jnp.int32, (rows, LANES), 1)
    for h in range(ratio):
        piece = jnp.broadcast_to(column[h * rows : (h + 1) * rows, :], (rows, LANES))
        into = jnp.where(lane == first + h, piece, into)
    return into


def lanes_to_heads(packed, ratio, first):
    return jnp.concatenate([packed[:, first + h : first + h + 1] for h in range(ratio)], axis=0)


def kernel(
    distances,
    ratio,
    route_ref,
    block_len_ref,
    prefix_len_ref,
    deferred_ref,
    q_ref,
    bk_ref,
    bv_ref,
    ck_hbm,
    cv_hbm,
    out_ref,
    ck,
    cv,
    q_out,
    q_in,
    top_out,
    top_in,
    sum_out,
    sum_in,
    stat_out,
    stat_in,
    inner,
    mixed,
    cache_sem,
    q_sem,
    top_sem,
    sum_sem,
    stat_sem,
):
    peers = lax.axis_size("req")
    me = lax.axis_index("req")
    hops, rows = q_ref.shape[0], q_ref.shape[1]
    groups = bk_ref.shape[2] // HEAD_DIM
    cache_rows = ck.shape[1]
    stacked = ratio * rows
    order = list(reversed(range(hops)))
    holder = [lax.rem(me + distances[k], peers) for k in range(hops)]
    asker = [lax.rem(me + peers - distances[k], peers) for k in range(hops)]

    barrier = pltpu.get_barrier_semaphore()
    for k in range(hops):
        for peer in (holder[k], asker[k]):
            pl.semaphore_signal(barrier, inc=1, device_id={"req": peer}, device_id_type=MESH)

    loads = {}
    for k in order:
        loads[k] = [
            pltpu.make_async_copy(ck_hbm.at[k], ck.at[k], cache_sem.at[k, 0]),
            pltpu.make_async_copy(cv_hbm.at[k], cv.at[k], cache_sem.at[k, 1]),
        ]
        for load in loads[k]:
            load.start()

    block_of = []
    for k in range(hops):
        block = jnp.int32(0)
        for c in range(1, hops):
            block = jnp.where(route_ref[0, c] == k, jnp.int32(c), block)
        block_of.append(block)

    def send(source, target, sems, where, peer):
        return pltpu.make_async_remote_copy(
            src_ref=source.at[where],
            dst_ref=target.at[where],
            send_sem=sems.at[(0, *where)],
            recv_sem=sems.at[(1, *where)],
            device_id={"req": peer},
            device_id_type=MESH,
        )

    for k in order:
        for g in range(groups):
            for h in range(ratio):
                at = (g * ratio + h) * HEAD_DIM
                q_out[k, g, h * rows : (h + 1) * rows, :] = q_ref[block_of[k], :, at : at + HEAD_DIM]

    pl.semaphore_wait(barrier, 2 * hops)

    asks, tops, sums, stats = {}, {}, {}, {}
    for k in order:
        for g in range(groups):
            asks[k, g] = send(q_out, q_in, q_sem, (k, g), holder[k])
            asks[k, g].start()

    row = lax.rem(lax.broadcasted_iota(jnp.int32, (stacked, rows), 0), rows)
    column = lax.broadcasted_iota(jnp.int32, (stacked, rows), 1)
    for k in order:
        visible = (column <= row) & (column < block_len_ref[0, block_of[k]])
        packed = jnp.zeros((rows, LANES), jnp.float32)
        for g in range(groups):
            cols = slice(g * HEAD_DIM, (g + 1) * HEAD_DIM)
            scores = dot_nt(q_out[k, g], bk_ref[block_of[k], :, cols]) * SCALE
            scores = jnp.where(visible, scores, HIDDEN)
            inner[k, g] = scores
            packed = heads_to_lanes(
                jnp.max(scores, axis=1, keepdims=True), rows, ratio, g * ratio, packed
            )
        whole = jnp.concatenate([packed, jnp.zeros((LANES - rows, LANES), jnp.float32)], axis=0)
        top_out[k] = whole.T[: groups * ratio, :]
        tops[k] = send(top_out, top_in, top_sem, (k,), holder[k])
        tops[k].start()

    place = lax.broadcasted_iota(jnp.int32, (1, cache_rows), 1)
    pad = jnp.zeros((LANES - groups * ratio, LANES), jnp.float32)
    for k in order:
        bias = jnp.where(place < prefix_len_ref[0, k], 0.0, HIDDEN)
        for load in loads[k]:
            load.wait()
        tops[k].wait_recv()
        asked_top = jnp.concatenate([top_in[k], pad], axis=0).T[:rows, :]
        for g in range(groups):
            cols = slice(g * HEAD_DIM, (g + 1) * HEAD_DIM)
            asks[k, g].wait_recv()
            scores = dot_nt(q_in[k, g], ck[k, :, cols]) * SCALE + bias
            top = jnp.maximum(
                lanes_to_heads(asked_top, ratio, g * ratio), jnp.max(scores, axis=1, keepdims=True)
            )
            weights = jnp.exp2(scores - top)
            total = jnp.sum(weights, axis=1, keepdims=True)
            part = jnp.dot(
                weights.astype(jnp.bfloat16), cv[k, :, cols], preferred_element_type=jnp.float32
            )
            largest = jnp.maximum(jnp.max(jnp.abs(part), axis=1, keepdims=True), 1e-33)
            coded = jnp.round(part * (LEVELS / largest))
            sum_out[k, g] = coded.astype(jnp.int32).astype(jnp.int16)
            sums[k, g] = send(sum_out, sum_in, sum_sem, (k, g), asker[k])
            sums[k, g].start()
            zeros = jnp.zeros((rows, LANES), jnp.float32)
            upper = heads_to_lanes(top, rows, ratio, 0, zeros)
            upper = heads_to_lanes(largest, rows, ratio, ratio, upper)
            lower = heads_to_lanes(total, rows, ratio, 0, zeros)
            stat_out[k, g] = jnp.concatenate([upper, lower], axis=0).T[: 2 * ratio, :]
            stats[k, g] = send(stat_out, stat_in, stat_sem, (k, g), asker[k])
            stats[k, g].start()

    pad = jnp.zeros((LANES - 2 * ratio, LANES), jnp.float32)
    for k in order:
        continues = deferred_ref[0, block_of[k]] == 1
        live = row[:, :1] < block_len_ref[0, block_of[k]]
        for g in range(groups):
            cols = slice(g * HEAD_DIM, (g + 1) * HEAD_DIM)
            stats[k, g].wait_recv()
            packed = jnp.concatenate([stat_in[k, g], pad], axis=0).T
            scores = inner[k, g]
            top = jnp.where(
                continues, lanes_to_heads(packed[:rows], ratio, 0), jnp.max(scores, axis=1, keepdims=True)
            )
            outer_total = jnp.where(continues, lanes_to_heads(packed[rows:], ratio, 0), 0.0)
            step = jnp.where(continues, lanes_to_heads(packed[:rows], ratio, ratio) * (1.0 / LEVELS), 0.0)
            weights = jnp.exp2(scores - top)
            total = jnp.sum(weights, axis=1, keepdims=True) + outer_total
            part = jnp.dot(
                weights.astype(jnp.bfloat16), bv_ref[block_of[k], :, cols], preferred_element_type=jnp.float32
            )
            sums[k, g].wait_recv()
            part = part + sum_in[k, g].astype(jnp.int32).astype(jnp.float32) * step
            result = jnp.where(live, part / total, 0.0).astype(out_ref.dtype)
            for h in range(ratio):
                at = (g * ratio + h) * HEAD_DIM
                mixed[k, :, at : at + HEAD_DIM] = result[h * rows : (h + 1) * rows, :]

    for c in range(hops):
        out_ref[c] = mixed[route_ref[0, c]]

    for k in order:
        tops[k].wait_send()
        for g in range(groups):
            asks[k, g].wait_send()
            sums[k, g].wait_send()
            stats[k, g].wait_send()


def per_device(
    queries,
    block_keys,
    block_values,
    cache_keys,
    cache_values,
    block_len,
    prefix_len,
    deferred,
    route,
):
    peers = lax.axis_size("req")
    distances = (1, peers // 4, peers // 2)
    hops, rows, width = queries.shape
    cache_rows = cache_keys.shape[1]
    groups = block_keys.shape[2] // HEAD_DIM
    ratio = width // HEAD_DIM // groups
    stacked = ratio * rows
    smem = pl.BlockSpec(memory_space=pltpu.SMEM)
    vmem = pl.BlockSpec(memory_space=pltpu.VMEM)
    hbm = pl.BlockSpec(memory_space=pl.ANY)
    keys = rows + cache_rows
    return pl.pallas_call(
        functools.partial(kernel, distances, ratio),
        out_shape=jax.ShapeDtypeStruct(queries.shape, jnp.bfloat16),
        in_specs=[smem] * 4 + [vmem] * 3 + [hbm] * 2,
        out_specs=vmem,
        scratch_shapes=[
            pltpu.VMEM(cache_keys.shape, jnp.bfloat16),
            pltpu.VMEM(cache_values.shape, jnp.bfloat16),
            pltpu.VMEM((hops, groups, stacked, HEAD_DIM), jnp.bfloat16),
            pltpu.VMEM((hops, groups, stacked, HEAD_DIM), jnp.bfloat16),
            pltpu.VMEM((hops, groups * ratio, LANES), jnp.float32),
            pltpu.VMEM((hops, groups * ratio, LANES), jnp.float32),
            pltpu.VMEM((hops, groups, stacked, HEAD_DIM), jnp.int16),
            pltpu.VMEM((hops, groups, stacked, HEAD_DIM), jnp.int16),
            pltpu.VMEM((hops, groups, 2 * ratio, LANES), jnp.float32),
            pltpu.VMEM((hops, groups, 2 * ratio, LANES), jnp.float32),
            pltpu.VMEM((hops, groups, stacked, rows), jnp.float32),
            pltpu.VMEM((hops, rows, width), jnp.bfloat16),
            pltpu.SemaphoreType.DMA((hops, 2)),
            pltpu.SemaphoreType.DMA((2, hops, groups)),
            pltpu.SemaphoreType.DMA((2, hops)),
            pltpu.SemaphoreType.DMA((2, hops, groups)),
            pltpu.SemaphoreType.DMA((2, hops, groups)),
        ],
        compiler_params=pltpu.CompilerParams(
            collective_id=0, has_side_effects=True, vmem_limit_bytes=48 * 1024 * 1024
        ),
        cost_estimate=pl.CostEstimate(
            flops=4 * hops * rows * width * keys,
            bytes_accessed=4 * queries.size + 4 * cache_keys.size,
            transcendentals=hops * rows * width // HEAD_DIM * keys,
        ),
    )(route, block_len, prefix_len, deferred, queries, block_keys, block_values, cache_keys, cache_values)


def solution(mesh):
    return jax.shard_map(
        per_device,
        mesh=mesh,
        in_specs=(
            P(("parts", "req"), None, "tensor"),
            P(("parts", "req"), None, "tensor"),
            P(("parts", "req"), None, "tensor"),
            P(("parts", "req"), None, "tensor"),
            P(("parts", "req"), None, "tensor"),
            P(("parts", "req"), None),
            P(("parts", "req"), None),
            P(("parts", "req"), None),
            P(("parts", "req"), None),
        ),
        out_specs=P(("parts", "req"), None, "tensor"),
        check_vma=False,
    )
```

```python
import functools
import math

import jax
import jax.numpy as jnp
from jax import lax
from jax.experimental import pallas as pl
from jax.experimental.pallas import tpu as pltpu
from jax.sharding import PartitionSpec as P

HEAD_DIM = 128
LANES = 128
HIDDEN = -1e30
LEVELS = 32767.0
MESH = pl.DeviceIdType.MESH
SCALE = math.log2(math.e) / math.sqrt(HEAD_DIM)


def dot_nt(a, b):
    return lax.dot_general(a, b, (((1,), (1,)), ((), ())), preferred_element_type=jnp.float32)


def heads_to_lanes(column, rows, ratio, first, into):
    lane = lax.broadcasted_iota(jnp.int32, (rows, LANES), 1)
    for h in range(ratio):
        piece = jnp.broadcast_to(column[h * rows : (h + 1) * rows, :], (rows, LANES))
        into = jnp.where(lane == first + h, piece, into)
    return into


def lanes_to_heads(packed, ratio, first):
    return jnp.concatenate([packed[:, first + h : first + h + 1] for h in range(ratio)], axis=0)


def kernel(
    distances,
    ratio,
    route_hbm,
    block_len_hbm,
    prefix_len_hbm,
    deferred_hbm,
    q_hbm,
    bk_hbm,
    bv_hbm,
    ck_hbm,
    cv_hbm,
    out_hbm,
    route_ref,
    block_len_ref,
    prefix_len_ref,
    deferred_ref,
    q_ref,
    bk_ref,
    bv_ref,
    ck,
    cv,
    q_out,
    q_in,
    top_out,
    top_in,
    sum_out,
    sum_in,
    stat_out,
    stat_in,
    inner,
    mixed,
    small_sem,
    cache_sem,
    out_sem,
    q_sem,
    top_sem,
    sum_sem,
    stat_sem,
):
    peers = lax.axis_size("req")
    me = lax.axis_index("req")
    hops, rows = q_ref.shape[0], q_ref.shape[1]
    groups = bk_ref.shape[2] // HEAD_DIM
    cache_rows = ck.shape[1]
    stacked = ratio * rows
    order = list(reversed(range(hops)))
    steps = [(k, g) for g in range(groups) for k in order]
    holder = [lax.rem(me + distances[k], peers) for k in range(hops)]
    asker = [lax.rem(me + peers - distances[k], peers) for k in range(hops)]

    barrier = pltpu.get_barrier_semaphore()
    for k in range(hops):
        for peer in (holder[k], asker[k]):
            pl.semaphore_signal(barrier, inc=1, device_id={"req": peer}, device_id_type=MESH)

    small = [
        pltpu.make_async_copy(source, target, small_sem.at[i])
        for i, (source, target) in enumerate(
            [
                (q_hbm, q_ref),
                (route_hbm, route_ref),
                (block_len_hbm, block_len_ref),
                (bk_hbm, bk_ref),
                (prefix_len_hbm, prefix_len_ref),
                (deferred_hbm, deferred_ref),
                (bv_hbm, bv_ref),
            ]
        )
    ]
    for load in small:
        load.start()
    loads = {}
    for k in order:
        loads[k] = [
            pltpu.make_async_copy(ck_hbm.at[k], ck.at[k], cache_sem.at[k, 0]),
            pltpu.make_async_copy(cv_hbm.at[k], cv.at[k], cache_sem.at[k, 1]),
        ]
        for load in loads[k]:
            load.start()

    for load in small[:2]:
        load.wait()
    block_of = []
    for k in range(hops):
        block = jnp.int32(0)
        for c in range(1, hops):
            block = jnp.where(route_ref[0, c] == k, jnp.int32(c), block)
        block_of.append(block)

    def send(source, target, sems, where, peer):
        return pltpu.make_async_remote_copy(
            src_ref=source.at[where],
            dst_ref=target.at[where],
            send_sem=sems.at[(0, *where)],
            recv_sem=sems.at[(1, *where)],
            device_id={"req": peer},
            device_id_type=MESH,
        )

    asks, tops, sums, stats = {}, {}, {}, {}
    for k, g in steps:
        for h in range(ratio):
            at = (g * ratio + h) * HEAD_DIM
            q_out[k, g, h * rows : (h + 1) * rows, :] = q_ref[block_of[k], :, at : at + HEAD_DIM]
        if (k, g) == steps[0]:
            pl.semaphore_wait(barrier, 2 * hops)
        asks[k, g] = send(q_out, q_in, q_sem, (k, g), holder[k])
        asks[k, g].start()
    for load in small[2:]:
        load.wait()

    row = lax.rem(lax.broadcasted_iota(jnp.int32, (stacked, rows), 0), rows)
    column = lax.broadcasted_iota(jnp.int32, (stacked, rows), 1)
    for k in order:
        visible = (column <= row) & (column < block_len_ref[0, block_of[k]])
        packed = jnp.zeros((rows, LANES), jnp.float32)
        for g in range(groups):
            cols = slice(g * HEAD_DIM, (g + 1) * HEAD_DIM)
            scores = dot_nt(q_out[k, g], bk_ref[block_of[k], :, cols]) * SCALE
            scores = jnp.where(visible, scores, HIDDEN)
            inner[k, g] = scores
            packed = heads_to_lanes(
                jnp.max(scores, axis=1, keepdims=True), rows, ratio, g * ratio, packed
            )
        whole = jnp.concatenate([packed, jnp.zeros((LANES - rows, LANES), jnp.float32)], axis=0)
        top_out[k] = whole.T[: groups * ratio, :]
        tops[k] = send(top_out, top_in, top_sem, (k,), holder[k])
        tops[k].start()

    place = lax.broadcasted_iota(jnp.int32, (1, cache_rows), 1)
    pad = jnp.zeros((LANES - groups * ratio, LANES), jnp.float32)
    for k, g in steps:
        bias = jnp.where(place < prefix_len_ref[0, k], 0.0, HIDDEN)
        if k in loads:
            for load in loads.pop(k):
                load.wait()
            tops[k].wait_recv()
        asked_top = jnp.concatenate([top_in[k], pad], axis=0).T[:rows, :]
        cols = slice(g * HEAD_DIM, (g + 1) * HEAD_DIM)
        asks[k, g].wait_recv()
        scores = dot_nt(q_in[k, g], ck[k, :, cols]) * SCALE + bias
        top = jnp.maximum(
            lanes_to_heads(asked_top, ratio, g * ratio), jnp.max(scores, axis=1, keepdims=True)
        )
        weights = jnp.exp2(scores - top)
        total = jnp.sum(weights, axis=1, keepdims=True)
        part = jnp.dot(
            weights.astype(jnp.bfloat16), cv[k, :, cols], preferred_element_type=jnp.float32
        )
        largest = jnp.maximum(jnp.max(jnp.abs(part), axis=1, keepdims=True), 1e-33)
        coded = jnp.round(part * (LEVELS / largest))
        sum_out[k, g] = coded.astype(jnp.int32).astype(jnp.int16)
        sums[k, g] = send(sum_out, sum_in, sum_sem, (k, g), asker[k])
        sums[k, g].start()
        zeros = jnp.zeros((rows, LANES), jnp.float32)
        upper = heads_to_lanes(top, rows, ratio, 0, zeros)
        upper = heads_to_lanes(largest, rows, ratio, ratio, upper)
        lower = heads_to_lanes(total, rows, ratio, 0, zeros)
        stat_out[k, g] = jnp.concatenate([upper, lower], axis=0).T[: 2 * ratio, :]
        stats[k, g] = send(stat_out, stat_in, stat_sem, (k, g), asker[k])
        stats[k, g].start()

    pad = jnp.zeros((LANES - 2 * ratio, LANES), jnp.float32)
    for k, g in steps:
        continues = deferred_ref[0, block_of[k]] == 1
        live = row[:, :1] < block_len_ref[0, block_of[k]]
        cols = slice(g * HEAD_DIM, (g + 1) * HEAD_DIM)
        stats[k, g].wait_recv()
        packed = jnp.concatenate([stat_in[k, g], pad], axis=0).T
        scores = inner[k, g]
        top = jnp.where(
            continues, lanes_to_heads(packed[:rows], ratio, 0), jnp.max(scores, axis=1, keepdims=True)
        )
        outer_total = jnp.where(continues, lanes_to_heads(packed[rows:], ratio, 0), 0.0)
        step = jnp.where(continues, lanes_to_heads(packed[:rows], ratio, ratio) * (1.0 / LEVELS), 0.0)
        weights = jnp.exp2(scores - top)
        total = jnp.sum(weights, axis=1, keepdims=True) + outer_total
        part = jnp.dot(
            weights.astype(jnp.bfloat16), bv_ref[block_of[k], :, cols], preferred_element_type=jnp.float32
        )
        sums[k, g].wait_recv()
        part = part + sum_in[k, g].astype(jnp.int32).astype(jnp.float32) * step
        result = jnp.where(live, part / total, 0.0).astype(mixed.dtype)
        for h in range(ratio):
            at = (g * ratio + h) * HEAD_DIM
            mixed[k, :, at : at + HEAD_DIM] = result[h * rows : (h + 1) * rows, :]

    stores = []
    for c in range(hops):
        q_ref[c] = mixed[route_ref[0, c]]
        stores.append(pltpu.make_async_copy(q_ref.at[c], out_hbm.at[c], out_sem.at[c]))
        stores[c].start()

    for k in order:
        tops[k].wait_send()
        for g in range(groups):
            asks[k, g].wait_send()
            sums[k, g].wait_send()
            stats[k, g].wait_send()
    for store in stores:
        store.wait()


def per_device(
    queries,
    block_keys,
    block_values,
    cache_keys,
    cache_values,
    block_len,
    prefix_len,
    deferred,
    route,
):
    peers = lax.axis_size("req")
    distances = (1, peers // 4, peers // 2)
    hops, rows, width = queries.shape
    cache_rows = cache_keys.shape[1]
    groups = block_keys.shape[2] // HEAD_DIM
    ratio = width // HEAD_DIM // groups
    stacked = ratio * rows
    hbm = pl.BlockSpec(memory_space=pltpu.HBM)
    keys = rows + cache_rows
    return pl.pallas_call(
        functools.partial(kernel, distances, ratio),
        out_shape=jax.ShapeDtypeStruct(queries.shape, jnp.bfloat16),
        in_specs=[hbm] * 9,
        out_specs=hbm,
        scratch_shapes=[
            pltpu.SMEM(route.shape, jnp.int32),
            pltpu.SMEM(block_len.shape, jnp.int32),
            pltpu.SMEM(prefix_len.shape, jnp.int32),
            pltpu.SMEM(deferred.shape, jnp.int32),
            pltpu.VMEM(queries.shape, jnp.bfloat16),
            pltpu.VMEM(block_keys.shape, jnp.bfloat16),
            pltpu.VMEM(block_values.shape, jnp.bfloat16),
            pltpu.VMEM(cache_keys.shape, jnp.bfloat16),
            pltpu.VMEM(cache_values.shape, jnp.bfloat16),
            pltpu.VMEM((hops, groups, stacked, HEAD_DIM), jnp.bfloat16),
            pltpu.VMEM((hops, groups, stacked, HEAD_DIM), jnp.bfloat16),
            pltpu.VMEM((hops, groups * ratio, LANES), jnp.float32),
            pltpu.VMEM((hops, groups * ratio, LANES), jnp.float32),
            pltpu.VMEM((hops, groups, stacked, HEAD_DIM), jnp.int16),
            pltpu.VMEM((hops, groups, stacked, HEAD_DIM), jnp.int16),
            pltpu.VMEM((hops, groups, 2 * ratio, LANES), jnp.float32),
            pltpu.VMEM((hops, groups, 2 * ratio, LANES), jnp.float32),
            pltpu.VMEM((hops, groups, stacked, rows), jnp.float32),
            pltpu.VMEM((hops, rows, width), jnp.bfloat16),
            pltpu.SemaphoreType.DMA((7,)),
            pltpu.SemaphoreType.DMA((hops, 2)),
            pltpu.SemaphoreType.DMA((hops,)),
            pltpu.SemaphoreType.DMA((2, hops, groups)),
            pltpu.SemaphoreType.DMA((2, hops)),
            pltpu.SemaphoreType.DMA((2, hops, groups)),
            pltpu.SemaphoreType.DMA((2, hops, groups)),
        ],
        compiler_params=pltpu.CompilerParams(
            collective_id=0, has_side_effects=True, vmem_limit_bytes=64 * 1024 * 1024 - 65536
        ),
        cost_estimate=pl.CostEstimate(
            flops=4 * hops * rows * width * keys,
            bytes_accessed=4 * queries.size + 4 * cache_keys.size,
            transcendentals=hops * rows * width // HEAD_DIM * keys,
        ),
    )(route, block_len, prefix_len, deferred, queries, block_keys, block_values, cache_keys, cache_values)


def solution(mesh):
    return jax.shard_map(
        per_device,
        mesh=mesh,
        in_specs=(
            P(("parts", "req"), None, "tensor"),
            P(("parts", "req"), None, "tensor"),
            P(("parts", "req"), None, "tensor"),
            P(("parts", "req"), None, "tensor"),
            P(("parts", "req"), None, "tensor"),
            P(("parts", "req"), None),
            P(("parts", "req"), None),
            P(("parts", "req"), None),
            P(("parts", "req"), None),
        ),
        out_specs=P(("parts", "req"), None, "tensor"),
        check_vma=False,
    )
```

```python
import functools
import math

import jax
import jax.numpy as jnp
from jax import lax
from jax.experimental import pallas as pl
from jax.experimental.pallas import tpu as pltpu
from jax.sharding import PartitionSpec as P

HEAD_DIM = 128
LANES = 128
HIDDEN = -1e30
LEVELS = 32767.0
MESH = pl.DeviceIdType.MESH
SCALE = math.log2(math.e) / math.sqrt(HEAD_DIM)


def dot_nt(a, b):
    return lax.dot_general(a, b, (((1,), (1,)), ((), ())), preferred_element_type=jnp.float32)


def heads_to_lanes(column, rows, ratio, first, into):
    lane = lax.broadcasted_iota(jnp.int32, (rows, LANES), 1)
    for h in range(ratio):
        piece = jnp.broadcast_to(column[h * rows : (h + 1) * rows, :], (rows, LANES))
        into = jnp.where(lane == first + h, piece, into)
    return into


def lanes_to_heads(packed, ratio, first):
    return jnp.concatenate([packed[:, first + h : first + h + 1] for h in range(ratio)], axis=0)


def kernel(
    distances,
    ratio,
    route_hbm,
    block_len_hbm,
    prefix_len_hbm,
    deferred_hbm,
    q_hbm,
    bk_hbm,
    bv_hbm,
    ck_hbm,
    cv_hbm,
    out_hbm,
    route_ref,
    block_len_ref,
    prefix_len_ref,
    deferred_ref,
    q_ref,
    bk_ref,
    bv_ref,
    ck,
    cv,
    q_out,
    q_in,
    top_out,
    top_in,
    sum_out,
    sum_in,
    stat_out,
    stat_in,
    inner,
    mixed,
    small_sem,
    cache_sem,
    out_sem,
    q_sem,
    top_sem,
    sum_sem,
    stat_sem,
):
    peers = lax.axis_size("req")
    me = lax.axis_index("req")
    hops, rows = q_ref.shape[0], q_ref.shape[1]
    groups = bk_ref.shape[2] // HEAD_DIM
    cache_rows = ck.shape[1]
    stacked = ratio * rows
    order = list(reversed(range(hops)))
    steps = [(k, g) for g in range(groups) for k in order]
    holder = [lax.rem(me + distances[k], peers) for k in range(hops)]
    asker = [lax.rem(me + peers - distances[k], peers) for k in range(hops)]

    barrier = pltpu.get_barrier_semaphore()
    for k in range(hops):
        for peer in (holder[k], asker[k]):
            pl.semaphore_signal(barrier, inc=1, device_id={"req": peer}, device_id_type=MESH)

    small = [
        pltpu.make_async_copy(source, target, small_sem.at[i])
        for i, (source, target) in enumerate(
            [
                (q_hbm, q_ref),
                (route_hbm, route_ref),
                (block_len_hbm, block_len_ref),
                (bk_hbm, bk_ref),
                (prefix_len_hbm, prefix_len_ref),
                (deferred_hbm, deferred_ref),
                (bv_hbm, bv_ref),
            ]
        )
    ]
    for load in small:
        load.start()
    loads = {}
    for k in order:
        loads[k] = [
            pltpu.make_async_copy(ck_hbm.at[k], ck.at[k], cache_sem.at[k, 0]),
            pltpu.make_async_copy(cv_hbm.at[k], cv.at[k], cache_sem.at[k, 1]),
        ]
        for load in loads[k]:
            load.start()

    for load in small[:2]:
        load.wait()
    block_of = []
    for k in range(hops):
        block = jnp.int32(0)
        for c in range(1, hops):
            block = jnp.where(route_ref[0, c] == k, jnp.int32(c), block)
        block_of.append(block)

    def send(source, target, sems, where, peer):
        return pltpu.make_async_remote_copy(
            src_ref=source.at[where],
            dst_ref=target.at[where],
            send_sem=sems.at[(0, *where)],
            recv_sem=sems.at[(1, *where)],
            device_id={"req": peer},
            device_id_type=MESH,
        )

    asks, tops, sums, stats = {}, {}, {}, {}
    for k, g in steps:
        for h in range(ratio):
            at = (g * ratio + h) * HEAD_DIM
            q_out[k, g, h * rows : (h + 1) * rows, :] = q_ref[block_of[k], :, at : at + HEAD_DIM]
        if (k, g) == steps[0]:
            pl.semaphore_wait(barrier, 2 * hops)
        asks[k, g] = send(q_out, q_in, q_sem, (k, g), holder[k])
        asks[k, g].start()
    for load in small[2:]:
        load.wait()

    row = lax.rem(lax.broadcasted_iota(jnp.int32, (stacked, rows), 0), rows)
    column = lax.broadcasted_iota(jnp.int32, (stacked, rows), 1)
    for k in order:
        visible = (column <= row) & (column < block_len_ref[0, block_of[k]])
        packed = jnp.zeros((rows, LANES), jnp.float32)
        for g in range(groups):
            cols = slice(g * HEAD_DIM, (g + 1) * HEAD_DIM)
            scores = dot_nt(q_out[k, g], bk_ref[block_of[k], :, cols]) * SCALE
            scores = jnp.where(visible, scores, HIDDEN)
            inner[k, g] = scores
            packed = heads_to_lanes(
                jnp.max(scores, axis=1, keepdims=True), rows, ratio, g * ratio, packed
            )
        whole = jnp.concatenate([packed, jnp.zeros((LANES - rows, LANES), jnp.float32)], axis=0)
        top_out[k] = whole.T[: groups * ratio, :]
        tops[k] = send(top_out, top_in, top_sem, (k,), holder[k])
        tops[k].start()

    place = lax.broadcasted_iota(jnp.int32, (1, cache_rows), 1)
    pad = jnp.zeros((LANES - groups * ratio, LANES), jnp.float32)
    for k, g in steps:
        bias = jnp.where(place < prefix_len_ref[0, k], 0.0, HIDDEN)
        if k in loads:
            for load in loads.pop(k):
                load.wait()
            tops[k].wait_recv()
        asked_top = jnp.concatenate([top_in[k], pad], axis=0).T[:rows, :]
        cols = slice(g * HEAD_DIM, (g + 1) * HEAD_DIM)
        asks[k, g].wait_recv()
        scores = dot_nt(q_in[k, g], ck[k, :, cols]) * SCALE + bias
        top = jnp.maximum(
            lanes_to_heads(asked_top, ratio, g * ratio), jnp.max(scores, axis=1, keepdims=True)
        )
        weights = jnp.exp2(scores - top)
        total = jnp.sum(weights, axis=1, keepdims=True)
        part = jnp.dot(
            weights.astype(jnp.bfloat16), cv[k, :, cols], preferred_element_type=jnp.float32
        )
        largest = jnp.maximum(jnp.max(jnp.abs(part), axis=1, keepdims=True), 1e-33)
        coded = jnp.round(part * (LEVELS / largest))
        sum_out[k, g] = coded.astype(jnp.int32).astype(jnp.int16)
        zeros = jnp.zeros((rows, LANES), jnp.float32)
        upper = heads_to_lanes(top, rows, ratio, 0, zeros)
        upper = heads_to_lanes(largest, rows, ratio, ratio, upper)
        lower = heads_to_lanes(total, rows, ratio, 0, zeros)
        stat_out[k, g] = jnp.concatenate([upper, lower], axis=0).T[: 2 * ratio, :]
        stats[k, g] = send(stat_out, stat_in, stat_sem, (k, g), asker[k])
        stats[k, g].start()
        sums[k, g] = send(sum_out, sum_in, sum_sem, (k, g), asker[k])
        sums[k, g].start()

    pad = jnp.zeros((LANES - 2 * ratio, LANES), jnp.float32)
    for k, g in steps:
        continues = deferred_ref[0, block_of[k]] == 1
        live = row[:, :1] < block_len_ref[0, block_of[k]]
        cols = slice(g * HEAD_DIM, (g + 1) * HEAD_DIM)
        stats[k, g].wait_recv()
        packed = jnp.concatenate([stat_in[k, g], pad], axis=0).T
        scores = inner[k, g]
        top = jnp.where(
            continues, lanes_to_heads(packed[:rows], ratio, 0), jnp.max(scores, axis=1, keepdims=True)
        )
        outer_total = jnp.where(continues, lanes_to_heads(packed[rows:], ratio, 0), 0.0)
        step = jnp.where(continues, lanes_to_heads(packed[:rows], ratio, ratio) * (1.0 / LEVELS), 0.0)
        weights = jnp.exp2(scores - top)
        total = jnp.sum(weights, axis=1, keepdims=True) + outer_total
        part = jnp.dot(
            weights.astype(jnp.bfloat16), bv_ref[block_of[k], :, cols], preferred_element_type=jnp.float32
        )
        sums[k, g].wait_recv()
        part = part + sum_in[k, g].astype(jnp.int32).astype(jnp.float32) * step
        result = jnp.where(live, part / total, 0.0).astype(mixed.dtype)
        for h in range(ratio):
            at = (g * ratio + h) * HEAD_DIM
            mixed[k, :, at : at + HEAD_DIM] = result[h * rows : (h + 1) * rows, :]

    stores = []
    for c in range(hops):
        q_ref[c] = mixed[route_ref[0, c]]
        stores.append(pltpu.make_async_copy(q_ref.at[c], out_hbm.at[c], out_sem.at[c]))
        stores[c].start()

    for k in order:
        tops[k].wait_send()
        for g in range(groups):
            asks[k, g].wait_send()
            sums[k, g].wait_send()
            stats[k, g].wait_send()
    for store in stores:
        store.wait()


def per_device(
    queries,
    block_keys,
    block_values,
    cache_keys,
    cache_values,
    block_len,
    prefix_len,
    deferred,
    route,
):
    peers = lax.axis_size("req")
    distances = (1, peers // 4, peers // 2)
    hops, rows, width = queries.shape
    cache_rows = cache_keys.shape[1]
    groups = block_keys.shape[2] // HEAD_DIM
    ratio = width // HEAD_DIM // groups
    stacked = ratio * rows
    hbm = pl.BlockSpec(memory_space=pltpu.HBM)
    keys = rows + cache_rows
    return pl.pallas_call(
        functools.partial(kernel, distances, ratio),
        out_shape=jax.ShapeDtypeStruct(queries.shape, jnp.bfloat16),
        in_specs=[hbm] * 9,
        out_specs=hbm,
        scratch_shapes=[
            pltpu.SMEM(route.shape, jnp.int32),
            pltpu.SMEM(block_len.shape, jnp.int32),
            pltpu.SMEM(prefix_len.shape, jnp.int32),
            pltpu.SMEM(deferred.shape, jnp.int32),
            pltpu.VMEM(queries.shape, jnp.bfloat16),
            pltpu.VMEM(block_keys.shape, jnp.bfloat16),
            pltpu.VMEM(block_values.shape, jnp.bfloat16),
            pltpu.VMEM(cache_keys.shape, jnp.bfloat16),
            pltpu.VMEM(cache_values.shape, jnp.bfloat16),
            pltpu.VMEM((hops, groups, stacked, HEAD_DIM), jnp.bfloat16),
            pltpu.VMEM((hops, groups, stacked, HEAD_DIM), jnp.bfloat16),
            pltpu.VMEM((hops, groups * ratio, LANES), jnp.float32),
            pltpu.VMEM((hops, groups * ratio, LANES), jnp.float32),
            pltpu.VMEM((hops, groups, stacked, HEAD_DIM), jnp.int16),
            pltpu.VMEM((hops, groups, stacked, HEAD_DIM), jnp.int16),
            pltpu.VMEM((hops, groups, 2 * ratio, LANES), jnp.float32),
            pltpu.VMEM((hops, groups, 2 * ratio, LANES), jnp.float32),
            pltpu.VMEM((hops, groups, stacked, rows), jnp.float32),
            pltpu.VMEM((hops, rows, width), jnp.bfloat16),
            pltpu.SemaphoreType.DMA((7,)),
            pltpu.SemaphoreType.DMA((hops, 2)),
            pltpu.SemaphoreType.DMA((hops,)),
            pltpu.SemaphoreType.DMA((2, hops, groups)),
            pltpu.SemaphoreType.DMA((2, hops)),
            pltpu.SemaphoreType.DMA((2, hops, groups)),
            pltpu.SemaphoreType.DMA((2, hops, groups)),
        ],
        compiler_params=pltpu.CompilerParams(
            collective_id=0, has_side_effects=True, vmem_limit_bytes=64 * 1024 * 1024 - 65536
        ),
        cost_estimate=pl.CostEstimate(
            flops=4 * hops * rows * width * keys,
            bytes_accessed=4 * queries.size + 4 * cache_keys.size,
            transcendentals=hops * rows * width // HEAD_DIM * keys,
        ),
    )(route, block_len, prefix_len, deferred, queries, block_keys, block_values, cache_keys, cache_values)


def solution(mesh):
    return jax.shard_map(
        per_device,
        mesh=mesh,
        in_specs=(
            P(("parts", "req"), None, "tensor"),
            P(("parts", "req"), None, "tensor"),
            P(("parts", "req"), None, "tensor"),
            P(("parts", "req"), None, "tensor"),
            P(("parts", "req"), None, "tensor"),
            P(("parts", "req"), None),
            P(("parts", "req"), None),
            P(("parts", "req"), None),
            P(("parts", "req"), None),
        ),
        out_specs=P(("parts", "req"), None, "tensor"),
        check_vma=False,
    )
```
